256 devices in a mesh: expert: 64 (over y, z, core), replica: 4 (over x).
Axes of the slice: x: 4, y: 4, z: 8, core: 2. Of those that a mesh axis runs over, the one named last changes fastest.
Arguments:
- tokens: bfloat16 [8192, 4096], P('expert', 'replica'), may hold values from -6 to 6
- probs: float32 [8192, 8], P('expert'), may hold values from 0.02 to 0.3
- expert_ids: int32 [8192, 8], P('expert'), may hold values from 0 to 63, all different within a row; in each aligned block of 128 rows (0 to 127, 128 to 255, ...) at most 20 rows name the same one
- grad_out: bfloat16 [8192, 4096], P('expert', 'replica'), may hold values from -6 to 6
- w_gate: bfloat16 [64, 4096, 768], P('expert', 'replica'), may hold values from -0.09375 to 0.09375
- w_up: bfloat16 [64, 4096, 768], P('expert', 'replica'), may hold values from -0.09375 to 0.09375
- w_down: bfloat16 [64, 768, 4096], P('expert', None, 'replica'), may hold values from -0.21875 to 0.21875
Outputs:
- mixed: bfloat16 [8192, 4096], P('expert', 'replica')
- grad_tokens: bfloat16 [8192, 4096], P('expert', 'replica')
- grad_gate: bfloat16 [64, 4096, 768], P('expert', 'replica')
- grad_up: bfloat16 [64, 4096, 768], P('expert', 'replica')
- grad_down: bfloat16 [64, 768, 4096], P('expert', None, 'replica')
The draws below stay inside these ranges and needn't reach their ends.
Inputs may be any that keep to these rules, and one draw needn't show every extreme that they name: `expert_ids`: the 8 ids of a token differ. Among the entries of the 128 tokens of one index of the expert axis, no expert is named more than 20 times, a bound that some block reaches.
All inputs are finite; a program needn't handle non-finite values.
Results may differ from the reference program's by a relative error of at most 0.024.
Values may be sent and summed in bfloat16 or wider, within the bound.
No kernel may reach another device: no remote copies, remote signals or barrier semaphores. Data moves between devices by JAX's collectives and lax.ppermute only.
A program may use at most 128 MiB of HBM per device.

```python
import math
import jax
import jax.numpy as jnp
import numpy as np
from jax import lax

D = 4096
HID = 768
TOP = 8
TOK_DEV = 128
EXPERTS = 64
CAP = 20
TOKENS = 8192
N_EXPERT = 64
N_REPLICA = 4


def level_of(own_key, extent, shards, smallest, largest):
    level = 1.0
    for position, shards_of in shards:
        heights = jax.random.uniform(jax.random.fold_in(jax.random.fold_in(own_key, 6), position), (shards_of,), jnp.float32, smallest / len(shards), largest / len(shards))
        level = level * jnp.repeat(jnp.exp(heights), extent[position] // shards_of).reshape((-1,) + (1,) * (len(extent) - 1 - position))
    return level


def shared_out(rng, own, number, rows, count, top, most, slope):
    order = jax.random.permutation(rng, count)
    crowded, ordinary = load_shares(count, rows * top, most, slope, True), load_shares(count, rows * top, most, slope, False)
    places = jnp.arange(count)

    def named(sizes, turn):
        used = int((sizes > 0).sum())
        fixed = max(1, used // 4)
        shifted = fixed + (places - fixed + turn * (used - fixed)) % max(1, count - fixed)
        return jnp.zeros((count,), jnp.int32).at[order[jnp.where(places < fixed, places, shifted)]].set(jnp.asarray(sizes, jnp.int32))

    sizes = jnp.where(number % 4 == 0, named(crowded, number // 4), named(ordinary, number - number // 4 - 1))
    mixed = jax.random.permutation(jax.random.fold_in(own, 3), count)
    giver, taker = mixed[0:count // 2 * 2:2], mixed[1:count // 2 * 2:2]
    slack = jnp.minimum(sizes[giver] - 1, most - sizes[taker]) // 2
    slack = jnp.where((giver == order[0]) | (taker == order[0]) | (sizes[taker] == 0), 0, jnp.maximum(slack, 0))
    shifted = jax.random.randint(jax.random.fold_in(own, 4), (count // 2,), 0, 1 << 20) % (slack + 1)
    sizes = sizes.at[giver].add(-shifted).at[taker].add(shifted)
    items = jnp.searchsorted(jnp.cumsum(sizes), jnp.arange(rows * top), side="right").astype(jnp.int32)
    listing = items.reshape(top, rows).T
    listing = listing[jax.random.permutation(jax.random.fold_in(own, 1), rows)]
    turn = jax.random.randint(jax.random.fold_in(own, 2), (rows, 1), 0, top)
    return jnp.take_along_axis(listing, (jnp.arange(top)[None, :] + turn) % top, axis=1)


def load_shares(number_of, total, bound, lean, full):
    portions = [(1 << 20) // math.isqrt(rank ** lean) + 1 for rank in range(1, number_of + 1)]
    largest = bound if full else min(bound, max(-(-total // number_of), total * portions[0] // sum(portions)))
    least = 1 if total - largest >= number_of - 1 else 0
    counts, surplus = [largest] + [least] * (number_of - 1), total - largest - least * (number_of - 1)
    while surplus > 0:
        candidates = [i for i in range(1, number_of) if counts[i] < largest] or [i for i in range(1, number_of) if counts[i] < bound]
        mass, budget = sum([portions[i] for i in candidates]), surplus
        for i in candidates:
            extra = min(bound - counts[i], max(1, budget * portions[i] // mass), surplus)
            counts[i] = counts[i] + extra
            surplus = surplus - extra
    return np.array(counts)


def noise(stream_key, extent, spread, reach, cuts=(), kind=jnp.bfloat16):
    values = jax.random.normal(stream_key, extent, jnp.float32) * spread
    if len(cuts) > 0:
        values = level_of(stream_key, extent, cuts, -0.22, 0.18) * values
    return jnp.clip(values, min=-reach, max=reach).astype(kind)


def setup_inputs(seed: int = 0) -> dict:
    arg_keys = jax.random.split(jax.random.key(seed), 8)
    tokens = noise(arg_keys[0], (TOKENS, D), 1.0, 6.0, ((0, 64), (1, 4)))
    probs = jnp.clip(jnp.exp(math.log(0.3) - 2.7080503 * jax.random.uniform(arg_keys[1], (TOKENS, TOP), jnp.float32) ** level_of(arg_keys[1], (TOKENS, TOP), ((0, 64),), -0.2, 0.2)), 0.02, 0.3)
    expert_ids_keys = jax.random.split(jax.random.fold_in(arg_keys[2], 1), TOKENS // TOK_DEV)
    expert_ids_turns = jax.random.permutation(jax.random.fold_in(arg_keys[2], 3), TOKENS // TOK_DEV)
    expert_ids = jax.vmap(lambda own, number: shared_out(jax.random.fold_in(arg_keys[2], 2), own, number, TOK_DEV, EXPERTS, TOP, CAP, 2))(expert_ids_keys, expert_ids_turns).reshape((TOKENS, TOP))
    grad_out = noise(arg_keys[3], (TOKENS, D), 1.0, 6.0, ((0, 64), (1, 4)))
    w_gate = noise(arg_keys[4], (EXPERTS, D, HID), D ** -0.5, 0.09375, ((0, 64), (1, 4)))
    w_up = noise(arg_keys[5], (EXPERTS, D, HID), D ** -0.5, 0.09375, ((0, 64), (1, 4)))
    w_down = noise(arg_keys[6], (EXPERTS, HID, D), HID ** -0.5, 0.21875, ((0, 64), (2, 4)))
    return {"tokens": tokens, "probs": probs, "expert_ids": expert_ids, "grad_out": grad_out, "w_gate": w_gate, "w_up": w_up, "w_down": w_down}


def block_slots(block_ids):
    onehot = (block_ids[:, None] == jnp.arange(EXPERTS, dtype=jnp.int32)[None, :]).astype(jnp.int32)
    before = jnp.cumsum(onehot, axis=0) - onehot
    return jnp.sum(before * onehot, axis=1).astype(jnp.int32)


def split_sum(left, right):
    left_parts = left.astype(jnp.float32).reshape(left.shape[0], N_REPLICA, -1)
    right_parts = right.astype(jnp.float32).reshape(N_REPLICA, -1, right.shape[1])
    pieces = jnp.einsum("rpd,pdw->prw", left_parts, right_parts).astype(jnp.bfloat16)
    pieces = lax.optimization_barrier(pieces)
    return jnp.sum(pieces.astype(jnp.float32), axis=0)


def reference(tokens, probs, expert_ids, grad_out, w_gate, w_up, w_down):
    per_block = TOK_DEV * TOP
    block_ids = expert_ids.reshape(N_EXPERT, per_block).astype(jnp.int32)
    slots = jax.vmap(block_slots)(block_ids)
    column = (jnp.arange(N_EXPERT, dtype=jnp.int32)[:, None] * CAP + slots).reshape(-1)
    entries = jnp.arange(TOKENS * TOP, dtype=jnp.int32)
    flat_ids = block_ids.reshape(-1)
    table = jnp.zeros((EXPERTS, N_EXPERT * CAP), jnp.int32).at[flat_ids, column].set(entries)
    filled = jnp.zeros((EXPERTS, N_EXPERT * CAP), jnp.int32).at[flat_ids, column].set(1)
    flat_probs = probs.reshape(-1)
    contract = (((0,), (0,)), ((), ()))

    def one_expert(carry, inputs):
        mixed_acc, grad_acc = carry
        entry_row, live_row, gate_w, up_w, down_w = inputs
        token_index = (entry_row // TOP).astype(jnp.int32)
        live = live_row.astype(jnp.float32)
        row_prob = flat_probs[entry_row] * live
        row_data = tokens[token_index] * live[:, None].astype(tokens.dtype)
        gate_sum = split_sum(row_data, gate_w)
        up_sum = split_sum(row_data, up_w)
        hidden = (jax.nn.silu(gate_sum) * up_sum).astype(jnp.bfloat16)
        out_rows = jnp.dot(hidden, down_w, preferred_element_type=jnp.float32).astype(jnp.bfloat16)
        grad_rows = (grad_out[token_index].astype(jnp.float32) * row_prob[:, None]).astype(jnp.bfloat16)
        back_sum = split_sum(grad_rows, down_w.T)
        sigma = jax.nn.sigmoid(gate_sum)
        grad_a = (back_sum * up_sum * sigma * (1.0 + gate_sum * (1.0 - sigma))).astype(jnp.bfloat16)
        grad_b = (back_sum * jax.nn.silu(gate_sum)).astype(jnp.bfloat16)
        input_rows = (jnp.dot(grad_a, gate_w.T, preferred_element_type=jnp.float32)
                      + jnp.dot(grad_b, up_w.T, preferred_element_type=jnp.float32)).astype(jnp.bfloat16)
        grad_gate = lax.dot_general(row_data, grad_a, contract, preferred_element_type=jnp.float32).astype(jnp.bfloat16)
        grad_up = lax.dot_general(row_data, grad_b, contract, preferred_element_type=jnp.float32).astype(jnp.bfloat16)
        grad_down = lax.dot_general(hidden, grad_rows, contract, preferred_element_type=jnp.float32).astype(jnp.bfloat16)
        mixed_acc = mixed_acc.at[token_index].add(row_prob[:, None] * out_rows.astype(jnp.float32))
        grad_acc = grad_acc.at[token_index].add(input_rows.astype(jnp.float32))
        return (mixed_acc, grad_acc), (grad_gate, grad_up, grad_down)

    start = (jnp.zeros((TOKENS, D), jnp.float32), jnp.zeros((TOKENS, D), jnp.float32))
    (mixed_acc, grad_acc), (grad_gate, grad_up, grad_down) = lax.scan(
        one_expert, start, (table, filled, w_gate, w_up, w_down))
    return mixed_acc.astype(jnp.bfloat16), grad_acc.astype(jnp.bfloat16), grad_gate, grad_up, grad_down
```

```python
import jax
import jax.numpy as jnp
from jax import lax
from jax.sharding import Mesh, PartitionSpec as P

BF = jnp.bfloat16
F32 = jnp.float32
NY, NZ, NC, NX = 4, 8, 2, 4
CAP = 20
NEAR = (0, -1, 1, -2)
FAR = (2, -3, 3, 4)
SIZES = {"y": NY, "z": NZ, "core": NC, "x": NX}


def shift(value, axis, by):
    n = SIZES[axis]
    return lax.ppermute(value, axis, [(i, (i + by) % n) for i in range(n)])


def dot(a, b):
    return jnp.dot(a, b, preferred_element_type=F32)


def gather_ring(block):
    half = block.shape[0] // 2
    blocks = {0: block}
    up = down = block
    for step in range(1, 4):
        up, down = shift(up, "z", 1), shift(down, "z", -1)
        blocks[-step], blocks[step] = up, down
    blocks[4] = jnp.concatenate([shift(up[:half], "z", 1), shift(down[half:], "z", -1)], 0)
    return blocks


def sum_ring(parts):
    half = parts[0].shape[0] // 2

    def add(part, got):
        return (part + got.astype(F32))

    up = shift(parts[4][:half].astype(BF), "z", 1)
    down = shift(parts[4][half:].astype(BF), "z", -1)
    up = jnp.concatenate([add(parts[3][:half], up), parts[3][half:]], 0)
    down = jnp.concatenate([parts[-3][:half], add(parts[-3][half:], down)], 0)
    for step in (2, 1, 0):
        up = shift(up.astype(BF), "z", 1)
        down = shift(down.astype(BF), "z", -1)
        if step:
            up, down = add(parts[step], up), add(parts[-step], down)
    return (parts[0] + up.astype(F32) + down.astype(F32)).astype(BF)


def routing(probs, expert_ids):
    y, z, core = lax.axis_index("y"), lax.axis_index("z"), lax.axis_index("core")
    meta = jnp.concatenate([expert_ids.astype(F32).T, probs.T], 0)
    meta = jnp.broadcast_to(meta[None], (NZ * NC,) + meta.shape)
    meta = lax.all_to_all(meta, ("z", "core"), 0, 0, tiled=True)
    meta = meta.reshape(NZ, NC, 16, -1)
    offsets = jnp.array(NEAR + FAR, jnp.int32)
    meta = jnp.take(meta, (z + offsets) % NZ, axis=0)
    meta = jnp.take(meta, (core + jnp.arange(NC)) % NC, axis=1)
    ids, weight = meta[:, :, :8], meta[:, :, 8:]
    mine = ((((y + jnp.arange(NY)) % NY) * NZ + z) * NC + core).astype(F32)
    match = ids[None] == mine[:, None, None, None, None]
    member = jnp.any(match, axis=3)
    weight = jnp.sum(jnp.where(match, weight[None], 0.0), axis=3)
    tok = ids.shape[-1]
    earlier = (jnp.arange(tok)[:, None] < jnp.arange(tok)[None, :]).astype(BF)
    slot = dot(member.astype(BF).reshape(-1, tok), earlier).reshape(member.shape)
    slot = jnp.where(member, slot, -1000.0).astype(jnp.int32)
    def order(a):
        return a.reshape(NY, 2, 4, NC, tok).swapaxes(2, 3).reshape(NY, 2, 8, tok)

    slot, weight = order(slot), order(weight)
    place = slot + (jnp.arange(8, dtype=jnp.int32) * CAP)[None, None, :, None]
    return place.reshape(NY, 2, 8 * tok), weight.reshape(NY, 2, 8 * tok)


def chunk_of(blocks, offsets):
    own = jnp.concatenate([blocks[o] for o in offsets], 0)
    return jnp.concatenate([own, shift(own, "core", 1)], 0)


def spread(rows):
    return jnp.concatenate([rows[0]] + [shift(rows[s], "y", s) for s in range(1, NY)], 0)


def unspread(rows):
    return jnp.concatenate([rows[0]] + [shift(rows[s], "y", -s) for s in range(1, NY)], 0)


def sum_parts(part):
    rows = part.shape[0] // NX
    got = lax.all_to_all(part.reshape(NX, rows, -1), "x", 0, 0, tiled=True)
    return jnp.sum(got.astype(F32), axis=0)


def whole(quarter):
    got = lax.all_to_all(jnp.broadcast_to(quarter[None], (NX,) + quarter.shape), "x", 0, 0, tiled=True)
    return got.reshape(-1, quarter.shape[1])


def per_device(tokens, probs, expert_ids, grad_out, w_gate, w_up, w_down):
    gate_w, up_w, down_w = w_gate[0], w_up[0], w_down[0]
    hid = gate_w.shape[1]
    place, weight = routing(probs, expert_ids)
    token_blocks = gather_ring(tokens)
    grad_blocks = gather_ring(grad_out)
    chunks = []
    for c, offsets in enumerate((NEAR, FAR)):
        hot = place[:, c, None, :] == jnp.arange(8 * CAP, dtype=jnp.int32)[None, :, None]
        pick = hot.astype(BF).reshape(NY * 8 * CAP, -1)
        spots = jnp.sum(jnp.where(hot, weight[:, c, None, :], 0.0), axis=2).reshape(-1, 1)
        mix = jnp.where(hot, weight[:, c, None, :], 0.0).astype(BF).reshape(NY * 8 * CAP, -1)
        rows = spread(dot(pick, chunk_of(token_blocks, offsets)).astype(BF).reshape(NY, 8 * CAP, -1))
        gate, up = dot(rows, gate_w).astype(BF), dot(rows, up_w).astype(BF)
        sums = sum_parts(jnp.concatenate([gate, up], 1))
        chunks.append(dict(offsets=offsets, pick=pick, spots=spots, mix=mix, rows=rows, gate=sums[:, :hid], up=sums[:, hid:]))
    for c in chunks:
        grads = dot(c["pick"], chunk_of(grad_blocks, c["offsets"])) * c["spots"]
        c["grads"] = spread(grads.astype(BF).reshape(NY, 8 * CAP, -1))
    for c in chunks:
        c["hidden"] = whole((jax.nn.silu(c["gate"]) * c["up"]).astype(BF))
        back = sum_parts(dot(c["grads"], down_w.T).astype(BF))
        sigma = jax.nn.sigmoid(c["gate"])
        grad_a = (back * c["up"] * sigma * (1.0 + c["gate"] * (1.0 - sigma))).astype(BF)
        grad_b = (back * jax.nn.silu(c["gate"])).astype(BF)
        both = whole(jnp.concatenate([grad_a, grad_b], 1))
        c["grad_a"], c["grad_b"] = both[:, :hid], both[:, hid:]
    tok = tokens.shape[0]

    def give_back(rows, weights):
        rows = unspread(rows.astype(BF).reshape(NY, 8 * CAP, -1))
        part = lax.dot_general(weights, rows, (((0,), (0,)), ((), ())), preferred_element_type=F32)
        own, other = part[: 4 * tok], part[4 * tok :]
        own = own + shift(other.astype(BF), "core", 1).astype(F32)
        return [own[i * tok : (i + 1) * tok] for i in range(4)]

    mixed_parts, input_parts = {}, {}
    for c in chunks[::-1]:
        out_rows = dot(c["hidden"], down_w)
        mixed_parts.update(zip(c["offsets"], give_back(out_rows, c["mix"])))
    mixed = sum_ring(mixed_parts)
    for c in chunks[::-1]:
        input_rows = dot(c["grad_a"], gate_w.T) + dot(c["grad_b"], up_w.T)
        input_parts.update(zip(c["offsets"], give_back(input_rows, c["pick"])))
    grad_tokens = sum_ring(input_parts)

    def outer(left, right):
        left = jnp.concatenate([c[left] for c in chunks], 0)
        right = jnp.concatenate([c[right] for c in chunks], 0)
        contract = (((0,), (0,)), ((), ()))
        return lax.dot_general(left, right, contract, preferred_element_type=F32).astype(BF)[None]

    return (mixed, grad_tokens, outer("rows", "grad_a"), outer("rows", "grad_b"), outer("hidden", "grads"))


def solution(mesh):
    split = Mesh(mesh.devices.reshape(NY, NZ, NC, NX), ("y", "z", "core", "x"))
    e, x = ("y", "z", "core"), "x"
    in_specs = (P(e, x), P(e, None), P(e, None), P(e, x), P(e, x, None), P(e, x, None), P(e, None, x))
    out_specs = (P(e, x), P(e, x), P(e, x, None), P(e, x, None), P(e, None, x))
    return jax.shard_map(per_device, mesh=split, in_specs=in_specs, out_specs=out_specs, check_vma=False)
```

```python
import jax
import jax.numpy as jnp
from jax import lax
from jax.experimental import pallas as pl
from jax.experimental.pallas import tpu as pltpu
from jax.sharding import Mesh, PartitionSpec as P

BF = jnp.bfloat16
F32 = jnp.float32
NY, NZ, NC, NX = 4, 8, 2, 4
DEST = NY * NC
CAP = 20
NEAR, FAR = (0, -1, 1, -2), (2, -3, 3, 4)
OFFSETS = NEAR + FAR
NB = 4
SLOTS = NB * CAP
ROWS = DEST * SLOTS
QUARTER = ROWS // NX
VMEM = 28 * 2**20


def shift(value, axis, by):
    n = {"y": NY, "z": NZ, "core": NC, "x": NX}[axis]
    return lax.ppermute(value, axis, [(i, (i + by) % n) for i in range(n)])


def dot(a, b, contract=((1,), (0,))):
    return lax.dot_general(a, b, (contract, ((), ())), preferred_element_type=F32)


def call(body, outs, args, scratch=(), smem=(), macs=0):
    nbytes = sum(a.size * a.dtype.itemsize for a in list(args) + list(outs))
    specs = [
        pl.BlockSpec(memory_space=pltpu.SMEM if i in smem else pltpu.VMEM) for i in range(len(args))
    ]
    return pl.pallas_call(
        body,
        out_shape=outs,
        in_specs=specs,
        out_specs=[pl.BlockSpec(memory_space=pltpu.VMEM)] * len(outs),
        scratch_shapes=list(scratch),
        compiler_params=pltpu.CompilerParams(vmem_limit_bytes=VMEM),
        cost_estimate=pl.CostEstimate(flops=2 * macs, bytes_accessed=nbytes, transcendentals=0),
    )(*args)


def struct(shape, dtype=BF):
    return jax.ShapeDtypeStruct(shape, dtype)


def part_at(x, step, size):
    return pl.ds(pl.multiple_of(lax.rem(x + step, NX) * size, size), size)


def hot_rows(place_ref, hot_ref, weight_ref=None, scale_ref=None):
    slots, wide = hot_ref.shape[0] // DEST, hot_ref.shape[1]
    for d in range(DEST):
        part = pl.ds(d * slots, slots)
        hot = place_ref[d][None, :] == lax.broadcasted_iota(jnp.int32, (slots, wide), 0)
        hot_ref[part, :] = jnp.where(hot, 1.0, 0.0).astype(BF)
        if weight_ref is not None:
            weight = jnp.where(hot, weight_ref[d][None, :], 0.0)
            scale_ref[part, :] = jnp.sum(weight, axis=1, keepdims=True)


def pick_body(place_ref, data_ref, near_ref, far_ref, hot_ref):
    for c, out_ref in enumerate((near_ref, far_ref)):
        for d in range(DEST):
            spot = lax.broadcasted_iota(jnp.int32, (SLOTS, data_ref.shape[0]), 0) + c * SLOTS
            hot_ref[pl.ds(d * SLOTS, SLOTS), :] = jnp.where(place_ref[d][None, :] == spot, 1.0, 0.0).astype(BF)
        out_ref[...] = dot(hot_ref[...], data_ref[...]).astype(BF)


def pick_scaled_body(place_ref, weight_ref, data_ref, out_ref, hot_ref, scale_ref):
    hot_rows(place_ref, hot_ref, weight_ref, scale_ref)
    out_ref[...] = (dot(hot_ref[...], data_ref[...]) * scale_ref[...]).astype(BF)


def mixed_rows(place, weight, rows_ref):
    tokens, rows = place.shape[0], rows_ref.shape[0]
    slots = rows // DEST
    owner = lax.broadcasted_iota(jnp.int32, (DEST, rows), 1) // slots
    spread = jnp.where(owner == lax.broadcasted_iota(jnp.int32, (DEST, rows), 0), 1.0, 0.0).astype(BF)
    spot = (lax.broadcasted_iota(jnp.int32, (tokens, rows), 1) % slots).astype(F32)
    hot = dot(place, spread) == spot
    value = jnp.where(hot, 1.0 if weight is None else dot(weight, spread), 0.0)
    return dot(value.astype(BF), rows_ref[...])


def mix_out_body(place_ref, weight_ref, rows_ref, out_ref):
    half = out_ref.shape[0] // 2
    for c in range(2):
        part = pl.ds(c * half, half)
        out_ref[part, :] = mixed_rows(place_ref[part, :], weight_ref[part, :], rows_ref).astype(BF)


def mix_in_body(place_ref, rows_ref, *outs):
    sums = mixed_rows(place_ref[...], None, rows_ref).astype(BF)
    start = 0
    for out in outs:
        out[...] = sums[start : start + out.shape[0]]
        start += out.shape[0]


def roll_rows(x, rows_ref, turned_ref):
    size = rows_ref.shape[0] // NX
    for i in range(NX):
        turned_ref[pl.ds(i * size, size), :] = rows_ref[part_at(x, i, size), :]


def gate_up_body(x_ref, rows_ref, gate_ref, up_ref, *refs):
    outs, turned = refs[:NX], refs[NX]
    roll_rows(x_ref[0], rows_ref, turned)
    hid = gate_ref.shape[1]
    for n, w in enumerate((gate_ref, up_ref)):
        part = dot(turned[...], w[...]).astype(BF)
        for i in range(NX):
            outs[i][:, n * hid : (n + 1) * hid] = part[i * QUARTER : (i + 1) * QUARTER]


def hidden_body(a, b, c, d, sums_ref, hidden_ref):
    hid = hidden_ref.shape[1]
    sums = a[...].astype(F32) + b[...].astype(F32) + c[...].astype(F32) + d[...].astype(F32)
    sums_ref[...] = sums
    gate, up = sums[:, :hid], sums[:, hid:]
    hidden_ref[...] = (gate / (1.0 + jnp.exp(-gate)) * up).astype(BF)


def out_body(hidden_ref, down_ref, out_ref, order_ref):
    for q in range(NX):
        for c in range(2):
            for s in range(2):
                start = ((q * 2 + c) * 2 + s) * SLOTS
                to = ((q * 2 + s) * 2 + c) * SLOTS
                order_ref[pl.ds(to, SLOTS), :] = hidden_ref[pl.ds(start, SLOTS), :]
    out_ref[...] = dot(order_ref[...], down_ref[...]).astype(BF)


def back_body(x_ref, rows_ref, down_ref, *refs):
    outs, turned = refs[:NX], refs[NX]
    roll_rows(x_ref[0], rows_ref, turned)
    part = dot(turned[...], down_ref[...], ((1,), (1,))).astype(BF)
    size = rows_ref.shape[0] // NX
    for i in range(NX):
        outs[i][...] = part[i * size : (i + 1) * size]


def grads_body(a, b, c, d, near_ref, far_ref, *outs):
    hid = a.shape[1]
    sums = a[...].astype(F32) + b[...].astype(F32) + c[...].astype(F32) + d[...].astype(F32)
    for n, (sums_ref, both_ref) in enumerate(zip((near_ref, far_ref), outs)):
        for s in range(2):
            part = pl.ds(s * SLOTS, SLOTS)
            start = (s * 2 + n) * SLOTS
            back = sums[start : start + SLOTS]
            gate, up = sums_ref[part, :hid], sums_ref[part, hid:]
            sigma = 1.0 / (1.0 + jnp.exp(-gate))
            both_ref[part, :hid] = (back * up * sigma * (1.0 + gate * (1.0 - sigma))).astype(BF)
            both_ref[part, hid:] = (back * gate * sigma).astype(BF)


def input_body(x_ref, a, b, c, d, gate_ref, up_ref, rows_ref, both_ref):
    hid = gate_ref.shape[1]
    for i, piece in enumerate((a, b, c, d)):
        both_ref[part_at(x_ref[0], i, QUARTER), :] = piece[...]
    rows = dot(both_ref[:, :hid], gate_ref[...], ((1,), (1,)))
    rows_ref[...] = (rows + dot(both_ref[:, hid:], up_ref[...], ((1,), (1,)))).astype(BF)


def outer_body(rows_a, rows_b, both_a, both_b, gate_ref, up_ref):
    hid = gate_ref.shape[1]
    for n, out in enumerate((gate_ref, up_ref)):
        part = slice(n * hid, (n + 1) * hid)
        grad = dot(rows_a[...], both_a[:, part], ((0,), (0,)))
        out[...] = (grad + dot(rows_b[...], both_b[:, part], ((0,), (0,)))).astype(BF)


def routing(probs, expert_ids):
    z = lax.axis_index("z")
    top = expert_ids.shape[1]
    meta = jnp.concatenate([expert_ids.astype(F32).T, probs.T], 0)
    meta = jnp.broadcast_to(meta[None], (NZ,) + meta.shape)
    meta = lax.all_to_all(meta, "z", 0, 0, tiled=True)
    ids, weight = meta[:, :top], meta[:, top:]
    dest = jnp.arange(DEST)
    mine = ((dest // NC * NZ + z) * NC + dest % NC).astype(F32)
    match = ids[None] == mine[:, None, None, None]
    member = jnp.any(match, axis=2)
    weight = jnp.sum(jnp.where(match, weight[None], 0.0), axis=2)
    tok = ids.shape[-1]
    earlier = (jnp.arange(tok)[:, None] < jnp.arange(tok)[None, :]).astype(BF)
    slot = dot(member.astype(BF).reshape(-1, tok), earlier).reshape(member.shape)
    return jnp.where(member, slot, -1000.0), weight


def after(value, *others):
    return lax.optimization_barrier((value,) + others)[0]


def plus(a, b):
    return (a.astype(F32) + b.astype(F32)).astype(BF)


def per_device(tokens, probs, expert_ids, grad_out, w_gate, w_up, w_down):
    gate_w, up_w, down_w = w_gate[0], w_up[0], w_down[0]
    width, hid = gate_w.shape
    tok = tokens.shape[0]
    wide = NB * tok
    x = lax.axis_index("x").astype(jnp.int32).reshape(1)
    z = lax.axis_index("z")

    half = tok // 2
    all_tokens = lax.all_gather(tokens, "z", axis=0, tiled=True)
    all_grads = lax.all_gather(after(grad_out, all_tokens), "z", axis=0, tiled=True)
    slot, weight = routing(probs, expert_ids)
    turn = jnp.array([OFFSETS.index((d + 3) % NZ - 3) for d in range(NZ)])
    turn = jnp.take(turn, (jnp.arange(NZ) - z) % NZ)
    place = (slot + (turn * CAP).astype(F32)[None, :, None]).reshape(DEST, NZ * tok)
    weight = weight.reshape(DEST, NZ * tok)
    in_order = jnp.take(slot, (z + jnp.array(OFFSETS)) % NZ, axis=1)
    in_order = (in_order + (jnp.arange(NZ) % NB * CAP).astype(F32)[None, :, None]).reshape(DEST, 2, wide)

    pick_macs = ROWS * wide * width
    mat_macs = ROWS * width * hid

    def swap(rows):
        size = rows.shape[0]
        return lax.all_to_all(rows.reshape(DEST, size // DEST, width), ("y", "core"), 0, 0, tiled=True).reshape(size, width)

    def exchange(pieces):
        return [pieces[0], shift(pieces[1], "x", 1), shift(pieces[2], "x", 2), shift(pieces[3], "x", -1)]

    near, far = {}, {}
    table = place.astype(jnp.int32)
    near["picked"], far["picked"] = call(
        pick_body,
        [struct((ROWS, width))] * 2,
        [table, all_tokens],
        [pltpu.VMEM((ROWS, 2 * wide), BF)],
        macs=4 * pick_macs,
    )
    near["rows"] = swap(near["picked"])
    far["rows"] = swap(after(far["picked"], near["rows"]))
    near["place"], far["place"] = in_order[:, 0], in_order[:, 1]

    def gate_up(k, turn):
        k["parts"] = call(
            gate_up_body,
            [struct((QUARTER, 2 * hid))] * NX,
            [after(x, turn), k["rows"], gate_w, up_w],
            [pltpu.VMEM((ROWS, width), BF)],
            smem=(0,),
            macs=2 * mat_macs,
        )
        k["pieces"] = exchange(k["parts"])

    def hide(k, turn):
        k["pieces"][0] = after(k["pieces"][0], turn)
        k["sums"], k["hidden"] = call(
            hidden_body,
            [struct((QUARTER, 2 * hid), F32), struct((QUARTER, hid))],
            k["pieces"],
        )

    gate_up(near, far["picked"])
    (picked,) = call(
        pick_scaled_body,
        [struct((2 * ROWS, width))],
        [after(table, near["parts"][0]), weight, all_grads],
        [pltpu.VMEM((2 * ROWS, 2 * wide), BF), pltpu.VMEM((2 * ROWS, 1), F32)],
        macs=4 * pick_macs,
    )
    grads = swap(after(picked, far["rows"]))
    gate_up(far, picked)
    hide(near, far["parts"][0])
    far["pieces"][0] = after(far["pieces"][0], grads)
    hide(far, near["hidden"])
    hidden = lax.all_gather(jnp.concatenate([near["hidden"], far["hidden"]], 0), "x", axis=0, tiled=True)
    pieces = call(
        back_body,
        [struct((2 * QUARTER, hid))] * NX,
        [after(x, far["hidden"]), grads, down_w],
        [pltpu.VMEM((2 * ROWS, width), BF)],
        smem=(0,),
        macs=2 * mat_macs,
    )
    near["both"], far["both"] = call(
        grads_body, [struct((QUARTER, 2 * hid))] * 2, exchange(pieces) + [near["sums"], far["sums"]]
    )
    picked, hidden = call(
        out_body,
        [struct((2 * ROWS, width)), struct((2 * ROWS, hid))],
        [after(hidden, far["both"]), down_w],
        macs=2 * mat_macs,
    )
    out_rows = swap(picked)

    def to_input(k, turn):
        both = k["both"]
        pieces = [both, shift(both, "x", -1), shift(both, "x", 2), shift(both, "x", 1)]
        k["input"], k["both"] = call(
            input_body,
            [struct((ROWS, width)), struct((ROWS, 2 * hid))],
            [after(x, turn)] + pieces + [gate_w, up_w],
            smem=(0,),
            macs=2 * mat_macs,
        )

    def mix_in(k, rows, sizes):
        return call(
            mix_in_body,
            [struct((n, width)) for n in sizes],
            [k["place"].T.astype(BF), rows],
            macs=pick_macs,
        )

    to_input(far, picked)
    far_rows = swap(after(far["input"], out_rows))
    (mixed,) = call(
        mix_out_body,
        [struct((NZ * tok, width))],
        [after(place.T.astype(BF), far["input"]), weight.T.astype(BF), out_rows],
        macs=4 * pick_macs,
    )
    sums = {1: mix_in(far, after(far_rows, mixed), [tok] * 3 + [tok // 2] * 2)}
    to_input(near, sums[1][0])
    mixed = lax.psum_scatter(mixed, "z", scatter_dimension=0, tiled=True)
    near_rows = swap(after(near["input"], far_rows))
    grad_gate, grad_up = call(
        outer_body,
        [struct((width, hid))] * 2,
        [after(near["rows"], near["input"]), far["rows"], near["both"], far["both"]],
        macs=4 * mat_macs,
    )
    grad_down = dot(after(hidden, near["input"]), grads, ((0,), (0,))).astype(BF)
    sums[0] = mix_in(near, after(near_rows, grad_gate), [tok] * 4)
    at_2, at_m3, at_3, low, high = sums[1]
    at_0, at_m1, at_1, at_m2 = sums[0]
    low, high = shift(low, "z", 1), shift(high, "z", -1)
    up = shift(jnp.concatenate([plus(at_3[:half], low), at_3[half:]], 0), "z", 1)
    down = shift(jnp.concatenate([at_m3[:half], plus(at_m3[half:], high)], 0), "z", -1)
    up = shift(plus(at_2, up), "z", 1)
    down = shift(plus(at_m2, down), "z", -1)
    up, down = shift(plus(at_1, up), "z", 1), shift(plus(at_m1, down), "z", -1)
    grad_tokens = (at_0.astype(F32) + up.astype(F32) + down.astype(F32)).astype(BF)

    return (mixed, grad_tokens, grad_gate[None], grad_up[None], grad_down[None])


def solution(mesh):
    split = Mesh(mesh.devices.reshape(NY, NZ, NC, NX), ("y", "z", "core", "x"))
    e, x = ("y", "z", "core"), "x"
    in_specs = (P(e, x), P(e, None), P(e, None), P(e, x), P(e, x, None), P(e, x, None), P(e, None, x))
    out_specs = (P(e, x), P(e, x), P(e, x, None), P(e, x, None), P(e, None, x))
    return jax.shard_map(per_device, mesh=split, in_specs=in_specs, out_specs=out_specs, check_vma=False)
```

```python
import jax
import jax.numpy as jnp
from jax import lax
from jax.experimental import pallas as pl
from jax.experimental.pallas import tpu as pltpu
from jax.sharding import Mesh, PartitionSpec as P

BF = jnp.bfloat16
F32 = jnp.float32
NY, NZ, NC, NX = 4, 8, 2, 4
DEST = NY * NC
CAP = 20
SLOTS = NZ * CAP
ROWS = DEST * SLOTS
QUARTER = ROWS // NX
TILE = 256
VMEM, MOST = 40 * 2**20, 60 * 2**20
OFFSETS = (0, -1, 1, -2, 2, -3, 3, 4)
NB = NZ // 2
PART = ROWS // 2


def shift(value, axis, by):
    n = {"y": NY, "z": NZ, "core": NC, "x": NX}[axis]
    return lax.ppermute(value, axis, [(i, (i + by) % n) for i in range(n)])


def after(value, *others):
    return lax.optimization_barrier((value,) + others)[0]


def dot(a, b, contract=((1,), (0,))):
    return lax.dot_general(a, b, (contract, ((), ())), preferred_element_type=F32)


def struct(shape, dtype=BF):
    return jax.ShapeDtypeStruct(shape, dtype)


def whole(a):
    return pl.BlockSpec(a.shape, lambda *_: (0,) * len(a.shape))


def columns(a):
    return pl.BlockSpec((a.shape[0], TILE), lambda i, *_: (0, i))


def rows_of(a, n):
    return pl.BlockSpec((a.shape[0] // n, a.shape[1]), lambda i, *_: (i, 0))


def turned_rows(a):
    return pl.BlockSpec((a.shape[0] // NX, a.shape[1]), lambda i, x: (lax.rem(x[0] + i, NX), 0))


def call(body, grid, args, in_specs, outs, out_specs, scratch=(), x=None, vmem=VMEM):
    spec = pltpu.PrefetchScalarGridSpec(
        num_scalar_prefetch=0 if x is None else 1,
        grid=(grid,),
        in_specs=in_specs,
        out_specs=out_specs,
        scratch_shapes=list(scratch),
    )
    return pl.pallas_call(
        body,
        out_shape=outs,
        grid_spec=spec,
        compiler_params=pltpu.CompilerParams(vmem_limit_bytes=vmem),
        cost_estimate=pl.CostEstimate(flops=1, bytes_accessed=1, transcendentals=0),
    )(*([] if x is None else [x]), *args)


def pick_body(scaled, place_ref, *refs):
    data_ref, out_ref, hot_ref, scale_ref = refs[-4:]
    for d in range(DEST):
        part = pl.ds(d * SLOTS, SLOTS)
        hot = place_ref[d][None, :] == lax.broadcasted_iota(jnp.int32, (SLOTS, hot_ref.shape[1]), 0)
        hot_ref[part, :] = jnp.where(hot, 1.0, 0.0).astype(BF)
        if scaled:
            weight = jnp.where(hot, refs[0][d][None, :], 0.0)
            scale_ref[part, :] = jnp.sum(weight, axis=1, keepdims=True)
    rows = dot(hot_ref[...], data_ref[...])
    out_ref[...] = (rows * scale_ref[...] if scaled else rows).astype(BF)


def pick(place, data, weight=None):
    args = [place, data] if weight is None else [place, weight, data]
    out = struct((ROWS, data.shape[1]))
    return call(
        lambda *refs: pick_body(weight is not None, *refs),
        1,
        args,
        [whole(a) for a in args],
        out,
        whole(out),
        [pltpu.VMEM((ROWS, data.shape[0]), BF), pltpu.VMEM((ROWS, 1), F32)],
    )


def mix_body(weighted, place_ref, *refs):
    rows_ref, out_ref = refs[-2:]
    rows = rows_ref.shape[0]
    slots = rows // DEST
    owner = lax.broadcasted_iota(jnp.int32, (DEST, rows), 1) // slots
    spread = jnp.where(owner == lax.broadcasted_iota(jnp.int32, (DEST, rows), 0), 1.0, 0.0).astype(BF)
    shape = (out_ref.shape[0], rows)
    spot = (lax.broadcasted_iota(jnp.int32, shape, 1) % slots).astype(F32)
    hot = dot(place_ref[...], spread) == spot
    value = jnp.where(hot, dot(refs[0][...], spread) if weighted else 1.0, 0.0)
    out_ref[...] = dot(value.astype(BF), rows_ref[...]).astype(BF)


def mix(place, rows, weight=None):
    tables = [t.T.astype(BF) for t in ([place] if weight is None else [place, weight])]
    tokens = tables[0].shape[0]
    out = struct((tokens, rows.shape[1]))
    return call(
        lambda *refs: mix_body(weight is not None, *refs),
        2,
        tables + [rows],
        [rows_of(t, 2) for t in tables] + [whole(rows)],
        out,
        rows_of(out, 2),
    )


def gate_up_body(rows_ref, gate_ref, up_ref, out_ref):
    tiles = pl.num_programs(0) // 2

    @pl.when(pl.program_id(0) < tiles)
    def _():
        out_ref[...] = dot(rows_ref[...], gate_ref[...]).astype(BF)

    @pl.when(pl.program_id(0) >= tiles)
    def _():
        out_ref[...] = dot(rows_ref[...], up_ref[...]).astype(BF)


def hidden_body(sums_ref, hidden_ref):
    hid = hidden_ref.shape[1]
    gate = sums_ref[:, :hid].astype(F32)
    hidden_ref[...] = (gate / (1.0 + jnp.exp(-gate)) * sums_ref[:, hid:].astype(F32)).astype(BF)


def back_body(x_ref, rows_ref, down_ref, *outs):
    part = dot(rows_ref[...], down_ref[...], ((1,), (1,))).astype(BF)
    for i, out in enumerate(outs):

        @pl.when(pl.program_id(0) == i)
        def _():
            out[...] = part


def grads_body(a, b, c, d, sums_ref, *outs):
    hid = a.shape[1]
    back = a[...].astype(F32) + b[...].astype(F32) + c[...].astype(F32) + d[...].astype(F32)
    gate, up = sums_ref[:, :hid].astype(F32), sums_ref[:, hid:].astype(F32)
    sigma = 1.0 / (1.0 + jnp.exp(-gate))
    grad_a = (back * up * sigma * (1.0 + gate * (1.0 - sigma))).astype(BF)
    grad_b = (back * gate * sigma).astype(BF)
    size = SLOTS // 2
    for n in range(QUARTER // size):
        out, part = outs[n % 2], pl.ds(n // 2 * size, size)
        out[part, :hid] = grad_a[n * size : (n + 1) * size]
        out[part, hid:] = grad_b[n * size : (n + 1) * size]


def out_body(hidden_ref, down_ref, out_ref):
    out_ref[...] = dot(hidden_ref[...], down_ref[...]).astype(BF)


def input_body(x_ref, *refs):
    pieces, (gate_w, up_w, rows_ref, both_ref) = refs[:NX], refs[NX:]
    hid = gate_w.shape[1]
    size = pieces[0].shape[0]
    for i, piece in enumerate(pieces):
        start = lax.rem(x_ref[0] + i, NX) * size
        both_ref[pl.ds(pl.multiple_of(start, size), size), :] = piece[...]
    rows = dot(both_ref[:, :hid], gate_w[...], ((1,), (1,))) + dot(both_ref[:, hid:], up_w[...], ((1,), (1,)))
    rows_ref[...] = rows.astype(BF)


def outer_body(left_ref, right_ref, out_ref):
    out_ref[...] = dot(left_ref[...], right_ref[...], ((0,), (0,))).astype(BF)


def outer(left, right):
    out = struct((left.shape[1], right.shape[1]))
    return call(
        outer_body, right.shape[1] // TILE, [left, right], [whole(left), columns(right)], out, columns(out)
    )


def outer_chunks_body(near_ref, far_ref, near_both, far_both, out_ref):
    width = near_ref.shape[2]
    near = dot(near_ref[...].reshape(PART, width), near_both[...], ((0,), (0,)))
    out_ref[...] = (near + dot(far_ref[...].reshape(PART, width), far_both[...], ((0,), (0,)))).astype(BF)


def outer_chunks(rows, near, far, tiles, skip):
    rows = rows.reshape(DEST, SLOTS, -1)
    out = struct((rows.shape[2], tiles * TILE))
    half = (DEST, SLOTS // 2, rows.shape[2])
    return call(
        outer_chunks_body,
        tiles,
        [rows, rows, near, far],
        [
            pl.BlockSpec(half, lambda i: (0, 0, 0)),
            pl.BlockSpec(half, lambda i: (0, 1, 0)),
            pl.BlockSpec((PART, TILE), lambda i: (0, i + skip)),
            pl.BlockSpec((PART, TILE), lambda i: (0, i + skip)),
        ],
        out,
        columns(out),
    )


def routing(probs, expert_ids):
    z = lax.axis_index("z")
    top = expert_ids.shape[1]
    meta = jnp.concatenate([expert_ids.astype(F32).T, probs.T], 0)
    meta = jnp.broadcast_to(meta[None], (NZ,) + meta.shape)
    meta = lax.all_to_all(meta, "z", 0, 0, tiled=True)
    ids, weight = meta[:, :top], meta[:, top:]
    dest = jnp.arange(DEST)
    mine = ((dest // NC * NZ + z) * NC + dest % NC).astype(F32)
    match = ids[None] == mine[:, None, None, None]
    member = jnp.any(match, axis=2)
    weight = jnp.sum(jnp.where(match, weight[None], 0.0), axis=2)
    tok = ids.shape[-1]
    earlier = (jnp.arange(tok)[:, None] < jnp.arange(tok)[None, :]).astype(BF)
    slot = dot(member.astype(BF).reshape(-1, tok), earlier).reshape(member.shape)
    return jnp.where(member, slot, -1000.0), weight


def plus(a, b):
    return (a.astype(F32) + b.astype(F32)).astype(BF)


def per_device(tokens, probs, expert_ids, grad_out, w_gate, w_up, w_down):
    gate_w, up_w, down_w = w_gate[0], w_up[0], w_down[0]
    width, hid = gate_w.shape
    tok = tokens.shape[0]
    x = lax.axis_index("x").astype(jnp.int32).reshape(1)
    z = lax.axis_index("z")

    def swap(rows):
        got = lax.all_to_all(rows.reshape(DEST, -1, width), ("y", "core"), 0, 0, tiled=True)
        return got.reshape(rows.shape)

    all_tokens = lax.all_gather(tokens, "z", axis=0, tiled=True)
    slot, weight = routing(probs, expert_ids)
    turn = jnp.array([OFFSETS.index((d + 3) % NZ - 3) for d in range(NZ)])
    turn = jnp.take(turn, (jnp.arange(NZ) - z) % NZ)
    place = (slot + (turn * CAP).astype(F32)[None, :, None]).reshape(DEST, NZ * tok)
    weight = weight.reshape(DEST, NZ * tok)
    listed = jnp.take(slot, (z + jnp.array(OFFSETS)) % NZ, axis=1)
    listed = listed + (jnp.arange(NZ) % NB * CAP).astype(F32)[None, :, None]
    near_place, far_place = (listed[:, c * NB : (c + 1) * NB].reshape(DEST, NB * tok) for c in range(2))
    table = place.astype(jnp.int32)
    all_grads = lax.all_gather(after(grad_out, all_tokens, table), "z", axis=0, tiled=True)

    rows = swap(pick(table, all_tokens))
    sums = struct((ROWS, 2 * hid))
    tiles = hid // TILE
    sums = call(
        gate_up_body,
        2 * tiles,
        [rows, gate_w, up_w],
        [
            whole(rows),
            pl.BlockSpec((width, TILE), lambda i: (0, jnp.minimum(i, tiles - 1))),
            pl.BlockSpec((width, TILE), lambda i: (0, jnp.maximum(i - tiles, 0))),
        ],
        sums,
        columns(sums),
    )
    picked = pick(after(table, sums), all_grads, weight)
    sums = lax.psum_scatter(sums, "x", scatter_dimension=0, tiled=True)
    grads = swap(picked)
    quarter = struct((QUARTER, hid))
    pieces = call(
        back_body,
        NX,
        [grads, down_w],
        [turned_rows(grads), whole(down_w)],
        [quarter] * NX,
        [whole(quarter)] * NX,
        x=x,
    )
    sums = after(sums, pieces[0])
    hidden = call(hidden_body, 1, [sums], [whole(sums)], quarter, whole(quarter))
    hidden = lax.all_gather(hidden, "x", axis=0, tiled=True)
    pieces = [pieces[0], shift(pieces[1], "x", 1), shift(pieces[2], "x", 2), shift(pieces[3], "x", -1)]
    out = struct((ROWS, width))
    out_rows = call(
        out_body,
        NX,
        [after(hidden, *pieces), down_w],
        [rows_of(hidden, NX), whole(down_w)],
        out,
        rows_of(out, NX),
        vmem=MOST,
    )
    mixed_rows = swap(out_rows)
    pieces[0] = after(pieces[0], out_rows)
    both = struct((QUARTER // 2, 2 * hid))
    near, far = call(
        grads_body, 1, pieces + [sums], [whole(p) for p in pieces] + [whole(sums)], [both] * 2, [whole(both)] * 2, vmem=MOST
    )
    near, far = ([own, shift(own, "x", -1), shift(own, "x", 2), shift(own, "x", 1)] for own in (near, far))

    def to_input(pieces, turn):
        out, both = struct((PART, width)), struct((PART, 2 * hid))
        return call(
            input_body,
            1,
            pieces + [gate_w, up_w],
            [whole(p) for p in pieces] + [whole(gate_w), whole(up_w)],
            [out, both],
            [whole(out), whole(both)],
            x=after(x, turn),
            vmem=MOST,
        )

    far_input, far = to_input(far, near[3])
    far_rows = swap(after(far_input, mixed_rows))
    mixed = mix(after(place, far_input), mixed_rows, weight)
    far_sums = mix(after(far_place, mixed), far_rows)
    near_input, near = to_input(near, far_sums)
    near_rows = swap(after(near_input, far_rows))
    mixed = lax.psum_scatter(mixed, "z", scatter_dimension=0, tiled=True)
    grad_gate = outer_chunks(rows, near, far, tiles, 0)
    grad_up = outer_chunks(rows, near, after(far, grad_gate), tiles, tiles)
    near_sums = mix(near_place, after(near_rows, grad_up))
    grad_down = outer(after(hidden, near_sums), grads)

    at = {o: far_sums[i * tok : (i + 1) * tok] for i, o in enumerate(OFFSETS[NB:])}
    at.update((o, near_sums[i * tok : (i + 1) * tok]) for i, o in enumerate(OFFSETS[:NB]))
    half = tok // 2
    low, high = shift(at[4][:half], "z", 1), shift(at[4][half:], "z", -1)
    up = shift(jnp.concatenate([plus(at[3][:half], low), at[3][half:]], 0), "z", 1)
    down = shift(jnp.concatenate([at[-3][:half], plus(at[-3][half:], high)], 0), "z", -1)
    for step in (2, 1):
        up, down = shift(plus(at[step], up), "z", 1), shift(plus(at[-step], down), "z", -1)
    grad_tokens = (at[0].astype(F32) + up.astype(F32) + down.astype(F32)).astype(BF)
    return (mixed, grad_tokens, grad_gate[None], grad_up[None], grad_down[None])


def solution(mesh):
    split = Mesh(mesh.devices.reshape(NY, NZ, NC, NX), ("y", "z", "core", "x"))
    e, x = ("y", "z", "core"), "x"
    in_specs = (P(e, x), P(e, None), P(e, None), P(e, x), P(e, x, None), P(e, x, None), P(e, None, x))
    out_specs = (P(e, x), P(e, x), P(e, x, None), P(e, x, None), P(e, None, x))
    return jax.shard_map(per_device, mesh=split, in_specs=in_specs, out_specs=out_specs, check_vma=False)
```

```python
import jax
import jax.numpy as jnp
from jax import lax
from jax.experimental import pallas as pl
from jax.experimental.pallas import tpu as pltpu
from jax.sharding import Mesh, PartitionSpec as P

BF = jnp.bfloat16
F32 = jnp.float32
NY, NZ, NC, NX = 4, 8, 2, 4
DEST = NY * NC
CAP = 20
SLOTS = NZ * CAP
ROWS = DEST * SLOTS
QUARTER = ROWS // NX
TILE = 256
VMEM, MOST = 40 * 2**20, 60 * 2**20
OFFSETS = (0, -1, 1, -2, 2, -3, 3, 4)
NB = NZ // 2
PART = ROWS // 2


def shift(value, axis, by):
    n = {"y": NY, "z": NZ, "core": NC, "x": NX}[axis]
    return lax.ppermute(value, axis, [(i, (i + by) % n) for i in range(n)])


def after(value, *others):
    return lax.optimization_barrier((value,) + others)[0]


def dot(a, b, contract=((1,), (0,))):
    return lax.dot_general(a, b, (contract, ((), ())), preferred_element_type=F32)


def struct(shape, dtype=BF):
    return jax.ShapeDtypeStruct(shape, dtype)


def whole(a):
    return pl.BlockSpec(a.shape, lambda *_: (0,) * len(a.shape))


def columns(a):
    return pl.BlockSpec((a.shape[0], TILE), lambda i, *_: (0, i))


def rows_of(a, n):
    return pl.BlockSpec((a.shape[0] // n, a.shape[1]), lambda i, *_: (i, 0))


def turned_rows(a):
    return pl.BlockSpec((a.shape[0] // NX, a.shape[1]), lambda i, x: (lax.rem(x[0] + i, NX), 0))


def call(body, grid, args, in_specs, outs, out_specs, scratch=(), x=None, vmem=VMEM):
    spec = pltpu.PrefetchScalarGridSpec(
        num_scalar_prefetch=0 if x is None else 1,
        grid=(grid,),
        in_specs=in_specs,
        out_specs=out_specs,
        scratch_shapes=list(scratch),
    )
    return pl.pallas_call(
        body,
        out_shape=outs,
        grid_spec=spec,
        compiler_params=pltpu.CompilerParams(vmem_limit_bytes=vmem),
        cost_estimate=pl.CostEstimate(flops=1, bytes_accessed=1, transcendentals=0),
    )(*([] if x is None else [x]), *args)


def pick_body(scaled, place_ref, *refs):
    data_ref, out_ref, hot_ref, scale_ref = refs[-4:]
    for d in range(DEST):
        part = pl.ds(d * SLOTS, SLOTS)
        hot = place_ref[d][None, :] == lax.broadcasted_iota(jnp.int32, (SLOTS, hot_ref.shape[1]), 0)
        hot_ref[part, :] = jnp.where(hot, 1.0, 0.0).astype(BF)
        if scaled:
            weight = jnp.where(hot, refs[0][d][None, :], 0.0)
            scale_ref[part, :] = jnp.sum(weight, axis=1, keepdims=True)
    rows = dot(hot_ref[...], data_ref[...])
    out_ref[...] = (rows * scale_ref[...] if scaled else rows).astype(BF)


def pick(place, data, weight=None):
    args = [place, data] if weight is None else [place, weight, data]
    out = struct((ROWS, data.shape[1]))
    return call(
        lambda *refs: pick_body(weight is not None, *refs),
        1,
        args,
        [whole(a) for a in args],
        out,
        whole(out),
        [pltpu.VMEM((ROWS, data.shape[0]), BF), pltpu.VMEM((ROWS, 1), F32)],
    )


def mix_body(weighted, place_ref, *refs):
    rows_ref, out_ref = refs[-2:]
    rows = rows_ref.shape[0]
    slots = rows // DEST
    owner = lax.broadcasted_iota(jnp.int32, (DEST, rows), 1) // slots
    spread = jnp.where(owner == lax.broadcasted_iota(jnp.int32, (DEST, rows), 0), 1.0, 0.0).astype(BF)
    shape = (out_ref.shape[0], rows)
    spot = (lax.broadcasted_iota(jnp.int32, shape, 1) % slots).astype(F32)
    hot = dot(place_ref[...], spread) == spot
    value = jnp.where(hot, dot(refs[0][...], spread) if weighted else 1.0, 0.0)
    out_ref[...] = dot(value.astype(BF), rows_ref[...]).astype(BF)


def mix(place, rows, weight=None):
    tables = [t.T.astype(BF) for t in ([place] if weight is None else [place, weight])]
    tokens = tables[0].shape[0]
    out = struct((tokens, rows.shape[1]))
    return call(
        lambda *refs: mix_body(weight is not None, *refs),
        2,
        tables + [rows],
        [rows_of(t, 2) for t in tables] + [whole(rows)],
        out,
        rows_of(out, 2),
    )


def gate_up_body(rows_ref, gate_ref, up_ref, out_ref):
    tiles = pl.num_programs(0) // 2

    @pl.when(pl.program_id(0) < tiles)
    def _():
        out_ref[...] = dot(rows_ref[...], gate_ref[...]).astype(BF)

    @pl.when(pl.program_id(0) >= tiles)
    def _():
        out_ref[...] = dot(rows_ref[...], up_ref[...]).astype(BF)


def hidden_body(sums_ref, hidden_ref):
    hid = hidden_ref.shape[1]
    gate = sums_ref[:, :hid].astype(F32)
    hidden_ref[...] = (gate / (1.0 + jnp.exp(-gate)) * sums_ref[:, hid:].astype(F32)).astype(BF)


def back_body(x_ref, rows_ref, down_ref, *outs):
    part = dot(rows_ref[...], down_ref[...], ((1,), (1,))).astype(BF)
    for i, out in enumerate(outs):

        @pl.when(pl.program_id(0) == i)
        def _():
            out[...] = part


def grads_body(a, b, c, d, sums_ref, *outs):
    hid = a.shape[1]
    back = a[...].astype(F32) + b[...].astype(F32) + c[...].astype(F32) + d[...].astype(F32)
    gate, up = sums_ref[:, :hid].astype(F32), sums_ref[:, hid:].astype(F32)
    sigma = 1.0 / (1.0 + jnp.exp(-gate))
    grad_a = (back * up * sigma * (1.0 + gate * (1.0 - sigma))).astype(BF)
    grad_b = (back * gate * sigma).astype(BF)
    size = SLOTS // 2
    for n in range(QUARTER // size):
        out, part = outs[n % 2], pl.ds(n // 2 * size, size)
        out[part, :hid] = grad_a[n * size : (n + 1) * size]
        out[part, hid:] = grad_b[n * size : (n + 1) * size]


def out_body(hidden_ref, down_ref, out_ref):
    out_ref[...] = dot(hidden_ref[...], down_ref[...]).astype(BF)


def input_body(x_ref, *refs):
    pieces, (gate_w, up_w, rows_ref, both_ref) = refs[:NX], refs[NX:]
    hid = gate_w.shape[1]
    size = pieces[0].shape[0]
    for i, piece in enumerate(pieces):
        start = lax.rem(x_ref[0] + i, NX) * size
        both_ref[pl.ds(pl.multiple_of(start, size), size), :] = piece[...]
    rows = dot(both_ref[:, :hid], gate_w[...], ((1,), (1,))) + dot(both_ref[:, hid:], up_w[...], ((1,), (1,)))
    rows_ref[...] = rows.astype(BF)


def outer_body(left_ref, right_ref, out_ref):
    out_ref[...] = dot(left_ref[...], right_ref[...], ((0,), (0,))).astype(BF)


def outer(left, right):
    out = struct((left.shape[1], right.shape[1]))
    return call(
        outer_body, right.shape[1] // TILE, [left, right], [whole(left), columns(right)], out, columns(out)
    )


def outer_chunks_body(near_ref, far_ref, near_both, far_both, out_ref):
    width = near_ref.shape[2]
    near = dot(near_ref[...].reshape(PART, width), near_both[...], ((0,), (0,)))
    out_ref[...] = (near + dot(far_ref[...].reshape(PART, width), far_both[...], ((0,), (0,)))).astype(BF)


def outer_chunks(rows, near, far, tiles, skip):
    rows = rows.reshape(DEST, SLOTS, -1)
    out = struct((rows.shape[2], tiles * TILE))
    half = (DEST, SLOTS // 2, rows.shape[2])
    return call(
        outer_chunks_body,
        tiles,
        [rows, rows, near, far],
        [
            pl.BlockSpec(half, lambda i: (0, 0, 0)),
            pl.BlockSpec(half, lambda i: (0, 1, 0)),
            pl.BlockSpec((PART, TILE), lambda i: (0, i + skip)),
            pl.BlockSpec((PART, TILE), lambda i: (0, i + skip)),
        ],
        out,
        columns(out),
    )


def routing(probs, expert_ids):
    z = lax.axis_index("z")
    top = expert_ids.shape[1]
    meta = jnp.concatenate([expert_ids.astype(F32).T, probs.T], 0)
    meta = jnp.broadcast_to(meta[None], (NZ,) + meta.shape)
    meta = lax.all_to_all(meta, "z", 0, 0, tiled=True)
    ids, weight = meta[:, :top], meta[:, top:]
    dest = jnp.arange(DEST)
    mine = ((dest // NC * NZ + z) * NC + dest % NC).astype(F32)
    match = ids[None] == mine[:, None, None, None]
    member = jnp.any(match, axis=2)
    weight = jnp.sum(jnp.where(match, weight[None], 0.0), axis=2)
    tok = ids.shape[-1]
    earlier = (jnp.arange(tok)[:, None] < jnp.arange(tok)[None, :]).astype(BF)
    slot = dot(member.astype(BF).reshape(-1, tok), earlier).reshape(member.shape)
    return jnp.where(member, slot, -1000.0), weight


def plus(a, b):
    return (a.astype(F32) + b.astype(F32)).astype(BF)


def per_device(tokens, probs, expert_ids, grad_out, w_gate, w_up, w_down):
    gate_w, up_w, down_w = w_gate[0], w_up[0], w_down[0]
    width, hid = gate_w.shape
    tok = tokens.shape[0]
    x = lax.axis_index("x").astype(jnp.int32).reshape(1)
    z = lax.axis_index("z")

    def swap(rows):
        got = lax.all_to_all(rows.reshape(DEST, -1, width), ("y", "core"), 0, 0, tiled=True)
        return got.reshape(rows.shape)

    all_tokens = lax.all_gather(tokens, "z", axis=0, tiled=True)
    slot, weight = routing(probs, expert_ids)
    turn = jnp.array([OFFSETS.index((d + 3) % NZ - 3) for d in range(NZ)])
    turn = jnp.take(turn, (jnp.arange(NZ) - z) % NZ)
    place = (slot + (turn * CAP).astype(F32)[None, :, None]).reshape(DEST, NZ * tok)
    weight = weight.reshape(DEST, NZ * tok)
    listed = jnp.take(slot, (z + jnp.array(OFFSETS)) % NZ, axis=1)
    listed = listed + (jnp.arange(NZ) % NB * CAP).astype(F32)[None, :, None]
    near_place, far_place = (listed[:, c * NB : (c + 1) * NB].reshape(DEST, NB * tok) for c in range(2))
    table = place.astype(jnp.int32)
    all_grads = lax.all_gather(after(grad_out, all_tokens, table), "z", axis=0, tiled=True)

    rows = swap(pick(table, all_tokens))
    sums = struct((ROWS, 2 * hid))
    tiles = hid // TILE
    sums = call(
        gate_up_body,
        2 * tiles,
        [rows, gate_w, up_w],
        [
            whole(rows),
            pl.BlockSpec((width, TILE), lambda i: (0, jnp.minimum(i, tiles - 1))),
            pl.BlockSpec((width, TILE), lambda i: (0, jnp.maximum(i - tiles, 0))),
        ],
        sums,
        columns(sums),
    )
    picked = pick(after(table, sums), all_grads, weight)
    sums = lax.psum_scatter(sums, "x", scatter_dimension=0, tiled=True)
    grads = swap(picked)
    quarter = struct((QUARTER, hid))
    sums = after(sums, grads)
    hidden = call(hidden_body, 1, [sums], [whole(sums)], quarter, whole(quarter))
    pieces = call(
        back_body,
        NX,
        [grads, down_w],
        [turned_rows(grads), whole(down_w)],
        [quarter] * NX,
        [whole(quarter)] * NX,
        x=after(x, hidden),
    )
    hidden = lax.all_gather(hidden, "x", axis=0, tiled=True)
    pieces = [pieces[0], shift(pieces[1], "x", 1), shift(pieces[2], "x", 2), shift(pieces[3], "x", -1)]
    out = struct((ROWS, width))
    out_rows = call(
        out_body,
        NX,
        [after(hidden, *pieces), down_w],
        [rows_of(hidden, NX), whole(down_w)],
        out,
        rows_of(out, NX),
        vmem=MOST,
    )
    mixed_rows = swap(out_rows)
    pieces[0] = after(pieces[0], out_rows)
    both = struct((QUARTER // 2, 2 * hid))
    near, far = call(
        grads_body, 1, pieces + [sums], [whole(p) for p in pieces] + [whole(sums)], [both] * 2, [whole(both)] * 2, vmem=MOST
    )
    near, far = ([own, shift(own, "x", -1), shift(own, "x", 2), shift(own, "x", 1)] for own in (near, far))

    def to_input(pieces, turn):
        out, both = struct((PART, width)), struct((PART, 2 * hid))
        return call(
            input_body,
            1,
            pieces + [gate_w, up_w],
            [whole(p) for p in pieces] + [whole(gate_w), whole(up_w)],
            [out, both],
            [whole(out), whole(both)],
            x=after(x, turn),
            vmem=MOST,
        )

    far_input, far = to_input(far, out_rows)
    far_rows = swap(after(far_input, mixed_rows))
    mixed = mix(after(place, far_input), mixed_rows, weight)
    far_sums = mix(after(far_place, mixed), far_rows)
    near_input, near = to_input(near, far_sums)
    near_rows = swap(after(near_input, far_rows))
    mixed = lax.psum_scatter(mixed, "z", scatter_dimension=0, tiled=True)
    grad_gate = outer_chunks(rows, near, far, tiles, 0)
    grad_up = outer_chunks(rows, near, after(far, grad_gate), tiles, tiles)
    near_sums = mix(after(near_place, grad_up), near_rows)
    grad_down = outer(after(hidden, near_sums), grads)

    at = {o: far_sums[i * tok : (i + 1) * tok] for i, o in enumerate(OFFSETS[NB:])}
    at.update((o, near_sums[i * tok : (i + 1) * tok]) for i, o in enumerate(OFFSETS[:NB]))
    half = tok // 2
    low, high = shift(at[4][:half], "z", 1), shift(at[4][half:], "z", -1)
    low, high = after(low, grad_up), after(high, grad_up)
    up = shift(jnp.concatenate([plus(at[3][:half], low), at[3][half:]], 0), "z", 1)
    down = shift(jnp.concatenate([at[-3][:half], plus(at[-3][half:], high)], 0), "z", -1)
    for step in (2, 1):
        up, down = shift(plus(at[step], up), "z", 1), shift(plus(at[-step], down), "z", -1)
    grad_tokens = (at[0].astype(F32) + up.astype(F32) + down.astype(F32)).astype(BF)
    return (mixed, grad_tokens, grad_gate[None], grad_up[None], grad_down[None])


def solution(mesh):
    split = Mesh(mesh.devices.reshape(NY, NZ, NC, NX), ("y", "z", "core", "x"))
    e, x = ("y", "z", "core"), "x"
    in_specs = (P(e, x), P(e, None), P(e, None), P(e, x), P(e, x, None), P(e, x, None), P(e, None, x))
    out_specs = (P(e, x), P(e, x), P(e, x, None), P(e, x, None), P(e, None, x))
    return jax.shard_map(per_device, mesh=split, in_specs=in_specs, out_specs=out_specs, check_vma=False)
```

```python
import jax
import jax.numpy as jnp
from jax import lax
from jax.experimental import pallas as pl
from jax.experimental.pallas import tpu as pltpu
from jax.sharding import Mesh, PartitionSpec as P

BF = jnp.bfloat16
F32 = jnp.float32
NY, NZ, NC, NX = 4, 8, 2, 4
DEST = NY * NC
CAP = 20
SLOTS = NZ * CAP
ROWS = DEST * SLOTS
QUARTER = ROWS // NX
TILE = 256
VMEM, MOST = 40 * 2**20, 60 * 2**20
OFFSETS = (0, -1, 1, -2, 2, -3, 3, 4)
NB = NZ // 2
PART = ROWS // 2


def shift(value, axis, by):
    n = {"y": NY, "z": NZ, "core": NC, "x": NX}[axis]
    return lax.ppermute(value, axis, [(i, (i + by) % n) for i in range(n)])


def after(value, *others):
    return lax.optimization_barrier((value,) + others)[0]


def dot(a, b, contract=((1,), (0,))):
    return lax.dot_general(a, b, (contract, ((), ())), preferred_element_type=F32)


def struct(shape, dtype=BF):
    return jax.ShapeDtypeStruct(shape, dtype)


def whole(a):
    return pl.BlockSpec(a.shape, lambda *_: (0,) * len(a.shape))


def columns(a):
    return pl.BlockSpec((a.shape[0], TILE), lambda i, *_: (0, i))


def rows_of(a, n):
    return pl.BlockSpec((a.shape[0] // n, a.shape[1]), lambda i, *_: (i, 0))


def turned_rows(a):
    return pl.BlockSpec((a.shape[0] // NX, a.shape[1]), lambda i, x: (lax.rem(x[0] + i, NX), 0))


def call(body, grid, args, in_specs, outs, out_specs, scratch=(), x=None, vmem=VMEM):
    spec = pltpu.PrefetchScalarGridSpec(
        num_scalar_prefetch=0 if x is None else 1,
        grid=(grid,),
        in_specs=in_specs,
        out_specs=out_specs,
        scratch_shapes=list(scratch),
    )
    return pl.pallas_call(
        body,
        out_shape=outs,
        grid_spec=spec,
        compiler_params=pltpu.CompilerParams(vmem_limit_bytes=vmem),
        cost_estimate=pl.CostEstimate(flops=1, bytes_accessed=1, transcendentals=0),
    )(*([] if x is None else [x]), *args)


def pick_body(scaled, place_ref, *refs):
    data_ref, out_ref, hot_ref, scale_ref = refs[-4:]
    for d in range(DEST):
        part = pl.ds(d * SLOTS, SLOTS)
        hot = place_ref[d][None, :] == lax.broadcasted_iota(jnp.int32, (SLOTS, hot_ref.shape[1]), 0)
        hot_ref[part, :] = jnp.where(hot, 1.0, 0.0).astype(BF)
        if scaled:
            weight = jnp.where(hot, refs[0][d][None, :], 0.0)
            scale_ref[part, :] = jnp.sum(weight, axis=1, keepdims=True)
    rows = dot(hot_ref[...], data_ref[...])
    out_ref[...] = (rows * scale_ref[...] if scaled else rows).astype(BF)


def pick(place, data, weight=None):
    args = [place, data] if weight is None else [place, weight, data]
    out = struct((ROWS, data.shape[1]))
    return call(
        lambda *refs: pick_body(weight is not None, *refs),
        1,
        args,
        [whole(a) for a in args],
        out,
        whole(out),
        [pltpu.VMEM((ROWS, data.shape[0]), BF), pltpu.VMEM((ROWS, 1), F32)],
    )


def mix_body(weighted, place_ref, *refs):
    rows_ref, out_ref = refs[-2:]
    rows = rows_ref.shape[0]
    slots = rows // DEST
    owner = lax.broadcasted_iota(jnp.int32, (DEST, rows), 1) // slots
    spread = jnp.where(owner == lax.broadcasted_iota(jnp.int32, (DEST, rows), 0), 1.0, 0.0).astype(BF)
    shape = (out_ref.shape[0], rows)
    spot = (lax.broadcasted_iota(jnp.int32, shape, 1) % slots).astype(F32)
    hot = dot(place_ref[...], spread) == spot
    value = jnp.where(hot, dot(refs[0][...], spread) if weighted else 1.0, 0.0)
    out_ref[...] = dot(value.astype(BF), rows_ref[...]).astype(BF)


def mix(place, rows, weight=None):
    tables = [t.T.astype(BF) for t in ([place] if weight is None else [place, weight])]
    tokens = tables[0].shape[0]
    out = struct((tokens, rows.shape[1]))
    return call(
        lambda *refs: mix_body(weight is not None, *refs),
        2,
        tables + [rows],
        [rows_of(t, 2) for t in tables] + [whole(rows)],
        out,
        rows_of(out, 2),
    )


def gate_up_body(rows_ref, gate_ref, up_ref, out_ref):
    tiles = pl.num_programs(0) // 2

    @pl.when(pl.program_id(0) < tiles)
    def _():
        out_ref[...] = dot(rows_ref[...], gate_ref[...]).astype(BF)

    @pl.when(pl.program_id(0) >= tiles)
    def _():
        out_ref[...] = dot(rows_ref[...], up_ref[...]).astype(BF)


def hidden_body(sums_ref, hidden_ref):
    hid = hidden_ref.shape[1]
    gate = sums_ref[:, :hid].astype(F32)
    hidden_ref[...] = (gate / (1.0 + jnp.exp(-gate)) * sums_ref[:, hid:].astype(F32)).astype(BF)


def back_body(x_ref, rows_ref, down_ref, *outs):
    part = dot(rows_ref[...], down_ref[...], ((1,), (1,))).astype(BF)
    for i, out in enumerate(outs):

        @pl.when(pl.program_id(0) == i)
        def _():
            out[...] = part


def grads_body(a, b, c, d, sums_ref, *outs):
    hid = a.shape[1]
    back = a[...].astype(F32) + b[...].astype(F32) + c[...].astype(F32) + d[...].astype(F32)
    gate, up = sums_ref[:, :hid].astype(F32), sums_ref[:, hid:].astype(F32)
    sigma = 1.0 / (1.0 + jnp.exp(-gate))
    grad_a = (back * up * sigma * (1.0 + gate * (1.0 - sigma))).astype(BF)
    grad_b = (back * gate * sigma).astype(BF)
    size = SLOTS // 2
    for n in range(QUARTER // size):
        out, part = outs[n % 2], pl.ds(n // 2 * size, size)
        out[part, :hid] = grad_a[n * size : (n + 1) * size]
        out[part, hid:] = grad_b[n * size : (n + 1) * size]


def out_body(hidden_ref, down_ref, out_ref):
    out_ref[...] = dot(hidden_ref[...], down_ref[...]).astype(BF)


def input_body(x_ref, *refs):
    pieces, (gate_w, up_w, rows_ref, both_ref) = refs[:NX], refs[NX:]
    hid = gate_w.shape[1]
    size = pieces[0].shape[0]
    for i, piece in enumerate(pieces):
        start = lax.rem(x_ref[0] + i, NX) * size
        both_ref[pl.ds(pl.multiple_of(start, size), size), :] = piece[...]
    rows = dot(both_ref[:, :hid], gate_w[...], ((1,), (1,))) + dot(both_ref[:, hid:], up_w[...], ((1,), (1,)))
    rows_ref[...] = rows.astype(BF)


def outer_body(left_ref, right_ref, out_ref):
    out_ref[...] = dot(left_ref[...], right_ref[...], ((0,), (0,))).astype(BF)


def outer(left, right):
    out = struct((left.shape[1], right.shape[1]))
    return call(
        outer_body, right.shape[1] // TILE, [left, right], [whole(left), columns(right)], out, columns(out)
    )


def outer_chunks_body(near_ref, far_ref, near_both, far_both, out_ref):
    width = near_ref.shape[2]
    near = dot(near_ref[...].reshape(PART, width), near_both[...], ((0,), (0,)))
    out_ref[...] = (near + dot(far_ref[...].reshape(PART, width), far_both[...], ((0,), (0,)))).astype(BF)


def outer_chunks(rows, near, far, tiles, skip):
    rows = rows.reshape(DEST, SLOTS, -1)
    out = struct((rows.shape[2], tiles * TILE))
    half = (DEST, SLOTS // 2, rows.shape[2])
    return call(
        outer_chunks_body,
        tiles,
        [rows, rows, near, far],
        [
            pl.BlockSpec(half, lambda i: (0, 0, 0)),
            pl.BlockSpec(half, lambda i: (0, 1, 0)),
            pl.BlockSpec((PART, TILE), lambda i: (0, i + skip)),
            pl.BlockSpec((PART, TILE), lambda i: (0, i + skip)),
        ],
        out,
        columns(out),
    )


def routing(probs, expert_ids):
    z = lax.axis_index("z")
    top = expert_ids.shape[1]
    meta = jnp.concatenate([expert_ids.astype(F32).T, probs.T], 0)
    meta = jnp.broadcast_to(meta[None], (NZ,) + meta.shape)
    meta = lax.all_to_all(meta, "z", 0, 0, tiled=True)
    ids, weight = meta[:, :top], meta[:, top:]
    dest = jnp.arange(DEST)
    mine = ((dest // NC * NZ + z) * NC + dest % NC).astype(F32)
    match = ids[None] == mine[:, None, None, None]
    member = jnp.any(match, axis=2)
    weight = jnp.sum(jnp.where(match, weight[None], 0.0), axis=2)
    tok = ids.shape[-1]
    earlier = (jnp.arange(tok)[:, None] < jnp.arange(tok)[None, :]).astype(BF)
    slot = dot(member.astype(BF).reshape(-1, tok), earlier).reshape(member.shape)
    return jnp.where(member, slot, -1000.0), weight


def plus(a, b):
    return (a.astype(F32) + b.astype(F32)).astype(BF)


def per_device(tokens, probs, expert_ids, grad_out, w_gate, w_up, w_down):
    gate_w, up_w, down_w = w_gate[0], w_up[0], w_down[0]
    width, hid = gate_w.shape
    tok = tokens.shape[0]
    x = lax.axis_index("x").astype(jnp.int32).reshape(1)
    z = lax.axis_index("z")

    def swap(rows):
        got = lax.all_to_all(rows.reshape(DEST, -1, width), ("y", "core"), 0, 0, tiled=True)
        return got.reshape(rows.shape)

    all_tokens = lax.all_gather(tokens, "z", axis=0, tiled=True)
    slot, weight = routing(probs, expert_ids)
    turn = jnp.array([OFFSETS.index((d + 3) % NZ - 3) for d in range(NZ)])
    turn = jnp.take(turn, (jnp.arange(NZ) - z) % NZ)
    place = (slot + (turn * CAP).astype(F32)[None, :, None]).reshape(DEST, NZ * tok)
    weight = weight.reshape(DEST, NZ * tok)
    listed = jnp.take(slot, (z + jnp.array(OFFSETS)) % NZ, axis=1)
    listed = listed + (jnp.arange(NZ) % NB * CAP).astype(F32)[None, :, None]
    near_place, far_place = (listed[:, c * NB : (c + 1) * NB].reshape(DEST, NB * tok) for c in range(2))
    table = place.astype(jnp.int32)
    all_grads = lax.all_gather(after(grad_out, all_tokens, table), "z", axis=0, tiled=True)

    rows = swap(pick(table, all_tokens))
    sums = struct((ROWS, 2 * hid))
    tiles = hid // TILE
    sums = call(
        gate_up_body,
        2 * tiles,
        [rows, gate_w, up_w],
        [
            whole(rows),
            pl.BlockSpec((width, TILE), lambda i: (0, jnp.minimum(i, tiles - 1))),
            pl.BlockSpec((width, TILE), lambda i: (0, jnp.maximum(i - tiles, 0))),
        ],
        sums,
        columns(sums),
    )
    picked = pick(after(table, sums), all_grads, weight)
    sums = lax.psum_scatter(sums, "x", scatter_dimension=0, tiled=True)
    grads = swap(picked)
    quarter = struct((QUARTER, hid))
    sums = after(sums, grads)
    hidden = call(hidden_body, 1, [sums], [whole(sums)], quarter, whole(quarter))
    pieces = call(
        back_body,
        NX,
        [grads, down_w],
        [turned_rows(grads), whole(down_w)],
        [quarter] * NX,
        [whole(quarter)] * NX,
        x=after(x, hidden),
    )
    hidden = lax.all_gather(hidden, "x", axis=0, tiled=True)
    pieces = [pieces[0], shift(pieces[1], "x", 1), shift(pieces[2], "x", 2), shift(pieces[3], "x", -1)]
    out = struct((ROWS, width))
    out_rows = call(
        out_body,
        NX,
        [after(hidden, *pieces), down_w],
        [rows_of(hidden, NX), whole(down_w)],
        out,
        rows_of(out, NX),
        vmem=MOST,
    )
    mixed_rows = swap(out_rows)
    pieces[0] = after(pieces[0], out_rows)
    both = struct((QUARTER // 2, 2 * hid))
    near, far = call(
        grads_body, 1, pieces + [sums], [whole(p) for p in pieces] + [whole(sums)], [both] * 2, [whole(both)] * 2, vmem=MOST
    )
    near, far = ([own, shift(own, "x", -1), shift(own, "x", 2), shift(own, "x", 1)] for own in (near, far))

    def to_input(pieces, turn):
        out, both = struct((PART, width)), struct((PART, 2 * hid))
        return call(
            input_body,
            1,
            pieces + [gate_w, up_w],
            [whole(p) for p in pieces] + [whole(gate_w), whole(up_w)],
            [out, both],
            [whole(out), whole(both)],
            x=after(x, turn),
        )

    far_input, far = to_input(far, out_rows)
    far_rows = swap(after(far_input, mixed_rows))
    mixed = mix(after(place, far_input), mixed_rows, weight)
    far_sums = mix(after(far_place, mixed), far_rows)
    near_input, near = to_input(near, far_sums)
    near_rows = swap(after(near_input, far_rows))
    mixed = lax.psum_scatter(mixed, "z", scatter_dimension=0, tiled=True)
    grad_gate = outer_chunks(rows, near, far, tiles, 0)
    grad_up = outer_chunks(rows, near, after(far, grad_gate), tiles, tiles)
    near_sums = mix(after(near_place, grad_up), near_rows)
    grad_down = outer(after(hidden, near_sums), grads)

    at = {o: far_sums[i * tok : (i + 1) * tok] for i, o in enumerate(OFFSETS[NB:])}
    at.update((o, near_sums[i * tok : (i + 1) * tok]) for i, o in enumerate(OFFSETS[:NB]))
    half = tok // 2
    low, high = shift(at[4][:half], "z", 1), shift(at[4][half:], "z", -1)
    low, high = after(low, grad_up), after(high, grad_up)
    up = shift(jnp.concatenate([plus(at[3][:half], low), at[3][half:]], 0), "z", 1)
    down = shift(jnp.concatenate([at[-3][:half], plus(at[-3][half:], high)], 0), "z", -1)
    for step in (2, 1):
        up, down = shift(plus(at[step], up), "z", 1), shift(plus(at[-step], down), "z", -1)
    grad_tokens = (at[0].astype(F32) + up.astype(F32) + down.astype(F32)).astype(BF)
    return (mixed, grad_tokens, grad_gate[None], grad_up[None], grad_down[None])


def solution(mesh):
    split = Mesh(mesh.devices.reshape(NY, NZ, NC, NX), ("y", "z", "core", "x"))
    e, x = ("y", "z", "core"), "x"
    in_specs = (P(e, x), P(e, None), P(e, None), P(e, x), P(e, x, None), P(e, x, None), P(e, None, x))
    out_specs = (P(e, x), P(e, x), P(e, x, None), P(e, x, None), P(e, None, x))
    return jax.shard_map(per_device, mesh=split, in_specs=in_specs, out_specs=out_specs, check_vma=False)
```
